32 devices in a mesh: groups: 2 (over y), vocab: 4 (over z), rows: 4 (over x, core).
Axes of the slice: x: 2, y: 2, z: 4, core: 2. Of those that a mesh axis runs over, the one named last changes fastest.
Arguments:
- student_hidden: bfloat16 [3584, 3072], P('vocab', ('groups', 'rows')), parts along dimension 1, may hold values from -180 to 180
- teacher_hidden: bfloat16 [5120, 3072], P('vocab', ('groups', 'rows')), parts along dimension 1, may hold values from -180 to 180
- teacher_head: bfloat16 [3, 5120, 512], P(None, None, 'vocab'), may hold values from -0.3125 to 0.3125
- student_head: bfloat16 [3584, 512], P(None, 'vocab'), may hold values from -0.3125 to 0.3125
- teacher_pick: int32 [3072], P(('groups', 'rows')), parts along dimension 0, may hold values from 0 to 2
- owner: int32 [8, 4], P('groups'), parts along dimension 0, may hold values from 0 to 3, as said below
Outputs:
- forward_kl: float32 [3072], P(('groups', 'rows')), parts along dimension 0
- reverse_kl: float32 [3072], P(('groups', 'rows')), parts along dimension 0
- grad_hidden: bfloat16 [3584, 3072], P('vocab', ('groups', 'rows')), parts along dimension 1
The draws below stay inside these ranges and needn't reach their ends.
There are 2 independent parts, one for each index of `groups`. The reference program is written for one: setup_inputs(seed, part) draws one part's arguments, and reference() takes and returns one part's arrays. A program takes and returns all parts, laid end to end along the dimension named above; an argument that names none is the same for every part. Nothing has to cross between parts.
Inputs may be any that keep to these rules, and one draw needn't show every extreme that they name: In each round, owner is a permutation of the row blocks; the 4 entries of each column are distinct, so no row block sends two sub-blocks to the same owner.
All inputs are finite; a program needn't handle non-finite values.
Results may differ from the reference program's by a relative error of at most 0.005.
Values may be sent and summed in bfloat16 or wider, within the bound.
A program may use at most 64 MiB of HBM per device.

```python
import jax
import jax.numpy as jnp
from jax import lax

D_T = 5120
D_S = 3584
TEACHERS = 3
ROUNDS = 4
ROWS = 1536
VOCAB = 512
SUB = 96
N_ROWS = 4


def scaled_rows(key, width):
    values = jnp.clip(jax.random.normal(key, (width, ROWS), jnp.float32), -6.0, 6.0)
    return values.astype(jnp.bfloat16)


def draw_student_hidden(key, part):
    key = jax.random.fold_in(key, 1)
    return scaled_rows(key, D_S)


def draw_teacher_hidden(key, part):
    key = jax.random.fold_in(key, 2)
    return scaled_rows(key, D_T)


def draw_owner(key, part):
    key = jax.random.fold_in(key, 3)
    relabel = jax.random.permutation(jax.random.fold_in(key, 1), N_ROWS).astype(jnp.int32)
    column_perm = jax.random.permutation(jax.random.fold_in(key, 2), N_ROWS).astype(jnp.int32)
    shifts = jax.random.permutation(jax.random.fold_in(key, 3), N_ROWS).astype(jnp.int32)[:ROUNDS]
    positions = (column_perm[None, :] + shifts[:, None]) % N_ROWS
    return relabel[positions].astype(jnp.int32)


def with_ends(array, stream_key, smallest, high):
    index_at = [jax.random.randint(jax.random.fold_in(stream_key, axis), (), 0, length) for axis, length in enumerate(array.shape)]
    longest = array.shape.index(max(array.shape))
    neighbour = index_at[:longest] + [(index_at[longest] + 1) % array.shape[longest]] + index_at[longest + 1:]
    return array.at[tuple(index_at)].set(smallest).at[tuple(neighbour)].set(high)


def block_scale(key, shape, cuts, least, largest):
    def one(position, shards_of):
        heights = jax.random.uniform(jax.random.fold_in(jax.random.fold_in(key, 6), position), (shards_of,), jnp.float32, least / len(cuts), largest / len(cuts))
        return jnp.repeat(jnp.exp(heights), shape[position] // shards_of).reshape((-1,) + (1,) * (len(shape) - position - 1))

    gain = one(*cuts[0])
    for cut in cuts[1:]:
        gain = gain * one(*cut)
    return gain


def normal_values(stream_key, shape, deviation, bound, cuts=(), held_as=jnp.bfloat16):
    result = jax.random.normal(stream_key, shape, jnp.float32) * deviation
    if len(cuts) > 0:
        result = block_scale(stream_key, shape, cuts, -0.22, 0.18) * result
    return jnp.clip(result, min=-bound, max=bound).astype(held_as)


def setup_inputs(seed: int = 0, part: int = 0) -> dict:
    streams_of = jax.random.split(jax.random.key(seed), 7)
    part_splits = jax.random.split(jax.random.fold_in(streams_of[6], part), 7)
    return {
        "student_hidden": draw_student_hidden(jax.random.fold_in(jax.random.fold_in(streams_of[6], part), 71), part),
        "teacher_hidden": draw_teacher_hidden(jax.random.fold_in(jax.random.fold_in(streams_of[6], part), 71), part),
        "teacher_head": normal_values(streams_of[2], (TEACHERS, D_T, VOCAB), (D_T // 16) ** -0.5, 0.3125, ((2, 4),)),
        "student_head": normal_values(streams_of[3], (D_S, VOCAB), (D_S // 9) ** -0.5, 0.3125, ((1, 4),)),
        "teacher_pick": with_ends(jax.random.randint(part_splits[4], (ROWS,), 0, 3), jax.random.fold_in(part_splits[4], 1), 0, 2).astype(jnp.int32),
        "owner": draw_owner(jax.random.fold_in(jax.random.fold_in(streams_of[6], part), 71), part),
    }


def route_rows(teacher_hidden, owner):
    width_t = teacher_hidden.shape[0]
    blocks_view = teacher_hidden.reshape(width_t, N_ROWS, ROUNDS, SUB)
    all_ranks = jnp.arange(N_ROWS, dtype=jnp.int32)
    matches = (owner[:, :, None] == all_ranks[None, None, :]).astype(jnp.int32)
    source = jnp.sum(matches * all_ranks[None, :, None], axis=1).astype(jnp.int32)
    round_ids = jnp.arange(ROUNDS, dtype=jnp.int32)
    moved = blocks_view[:, source.T, round_ids[None, :], :]
    return moved.reshape(width_t, ROWS)


def reference(student_hidden, teacher_hidden, teacher_head, student_head, teacher_pick, owner):
    routed = route_rows(teacher_hidden, owner)
    teacher_logits = jnp.zeros((ROWS, VOCAB), jnp.float32)
    for teacher in range(TEACHERS):
        pick_mask = (teacher_pick == teacher).astype(jnp.bfloat16)[None, :]
        teacher_logits = teacher_logits + lax.dot_general(routed * pick_mask, teacher_head[teacher], (((0,), (0,)), ((), ())), preferred_element_type=jnp.float32)
    student_logits = lax.dot_general(student_hidden, student_head, (((0,), (0,)), ((), ())), preferred_element_type=jnp.float32)
    log_teacher = teacher_logits - jax.nn.logsumexp(teacher_logits, axis=1, keepdims=True)
    log_student = student_logits - jax.nn.logsumexp(student_logits, axis=1, keepdims=True)
    p_teacher = jnp.exp(log_teacher)
    p_student = jnp.exp(log_student)
    forward_kl = jnp.sum(p_teacher * (log_teacher - log_student), axis=1)
    reverse_kl = jnp.sum(p_student * (log_student - log_teacher), axis=1)
    logit_grad = ((p_student - p_teacher) + p_student * (log_student - log_teacher - reverse_kl[:, None])).astype(jnp.bfloat16)
    grad_hidden = lax.dot_general(student_head, logit_grad, (((1,), (1,)), ((), ())), preferred_element_type=jnp.float32)
    return forward_kl, reverse_kl, grad_hidden.astype(jnp.bfloat16)
```

```python
import functools
import math

import jax
import jax.numpy as jnp
from jax import lax
from jax.experimental import pallas as pl
from jax.experimental.pallas import tpu as pltpu
from jax.sharding import PartitionSpec as P

MESH = pl.DeviceIdType.MESH
PART = jnp.float32
VALUE_BOUND = 180.0 * 0.3125


def part_scale(features):
    return 2.0 ** -max(0, math.ceil(math.log2(features * VALUE_BOUND / 60000.0)))


def window_kernel(
    nz,
    sub,
    sh_ref,
    th_ref,
    thead_ref,
    shead_ref,
    pick_ref,
    bmask_ref,
    smask_ref,
    kl_ref,
    grad_ref,
    wt,
    ws,
    sht,
    tht,
    own_t,
    own_s,
    send_t,
    send_s,
    recv_t,
    recv_s,
    tl_all,
    dz_all,
    kl_all,
    pick_all,
    local_sem,
    zs_sem,
    zr_sem,
    ps_sem,
    pr_sem,
    ks_sem,
    kr_sem,
    ls_sem,
    lr_sem,
    rs_sem,
    rr_sem,
    ds_sem,
    dr_sem,
):
    g = lax.axis_index("groups")
    z = lax.axis_index("vocab")
    r = lax.axis_index("rows")
    x, c = r // 2, r % 2
    rx = (1 - x) * 2 + c
    rp = x * 2 + (1 - c)
    ro = (1 - x) * 2 + (1 - c)
    gy = 1 - g
    dev_x, dev_y, dev_p = (g, z, rx), (gy, z, r), (g, z, rp)
    row_peers = (rp, rx, ro)
    own_p = (g * 4 + r, g * 4 + rx, gy * 4 + r, gy * 4 + rx)
    mate_p = (g * 4 + rp, g * 4 + ro, gy * 4 + rp, gy * 4 + ro)
    fwd_p = jnp.where(c == 0, own_p[1], own_p[2])
    fwd_dev = (jnp.where(c == 0, gy, g), z, jnp.where(c == 0, r, rx))

    ft, fs = th_ref.shape[0], sh_ref.shape[0]
    bt, bs = ft // 8, fs // 8
    vl = thead_ref.shape[2]

    def t_at(piece, zz):
        return wt.at[
            :, pl.ds(pl.multiple_of(piece * bt, bt), bt), pl.ds(pl.multiple_of(zz * vl, vl), vl)
        ]

    def s_at(piece, zz):
        return ws.at[
            pl.ds(pl.multiple_of(piece * bs, bs), bs), pl.ds(pl.multiple_of(zz * vl, vl), vl)
        ]

    at = (s_at, t_at)

    def remote(src, dst, ssem, rsem, dev):
        return pltpu.make_async_remote_copy(
            src_ref=src, dst_ref=dst, send_sem=ssem, recv_sem=rsem, device_id=dev, device_id_type=MESH
        )

    loc_t = pltpu.make_async_copy(
        thead_ref.at[:, pl.ds(pl.multiple_of(z * ft, ft), ft), :],
        wt.at[:, :, pl.ds(pl.multiple_of(z * vl, vl), vl)],
        local_sem.at[0],
    )
    loc_s = pltpu.make_async_copy(
        shead_ref.at[pl.ds(pl.multiple_of(z * fs, fs), fs), :],
        ws.at[:, pl.ds(pl.multiple_of(z * vl, vl), vl)],
        local_sem.at[1],
    )
    loc_s.start()
    loc_t.start()

    barrier = pltpu.get_barrier_semaphore()
    peers = [(g, (z + d) % nz, r) for d in range(1, nz)]
    peers += [(g, z, q) for q in row_peers] + [dev_y]
    for dev in peers:
        pl.semaphore_signal(barrier, inc=1, device_id=dev, device_id_type=MESH)
    pl.semaphore_wait(barrier, len(peers))

    sends = []

    def go(copy):
        copy.start()
        sends.append(copy)

    for a in range(2):
        for d in range(1, nz):
            zd = (z + d) % nz
            if a == 0:
                src = shead_ref.at[pl.ds(pl.multiple_of(zd * fs + own_p[0] * bs, bs), bs), :]
            else:
                src = thead_ref.at[:, pl.ds(pl.multiple_of(zd * ft + own_p[0] * bt, bt), bt), :]
            go(
                remote(
                    src, at[a](own_p[0], z), zs_sem.at[a, d - 1], zr_sem.at[a, d - 1], (g, zd, r)
                )
            )
    pick_all[r] = pick_ref[...]
    for i, q in enumerate(row_peers):
        go(remote(pick_all.at[r], pick_all.at[r], ks_sem.at[i], kr_sem.at[i], (g, z, q)))

    sht[...] = sh_ref[...].T
    tht[...] = th_ref[...].T

    def plane(a, d, kind, piece, dev):
        ref = at[a](piece, (z - d) % nz)
        return remote(ref, ref, ps_sem.at[a, d - 1, kind], pr_sem.at[a, d - 1, kind], dev)

    def stage1(a):
        for d in range(1, nz):
            zd = (z - d) % nz
            dst = at[a](own_p[0], zd)
            remote(dst, dst, zs_sem.at[a, d - 1], zr_sem.at[a, d - 1], (g, zd, r)).wait_recv()
            go(plane(a, d, 0, own_p[0], dev_x))
            go(plane(a, d, 1, own_p[0], dev_y))
            go(plane(a, d, 3, own_p[0], dev_p))

    def stage2(a):
        for d in range(1, nz):
            plane(a, d, 0, own_p[1], dev_x).wait_recv()
            plane(a, d, 1, own_p[2], dev_y).wait_recv()
            go(plane(a, d, 2, fwd_p, fwd_dev))
            go(plane(a, d, 4, own_p[1], dev_p))
            go(plane(a, d, 5, own_p[2], dev_p))

    def stage3(a):
        for d in range(1, nz):
            plane(a, d, 2, own_p[3], dev_x).wait_recv()
            go(plane(a, d, 6, own_p[3], dev_p))

    def stage4(a):
        for d in range(1, nz):
            for i in range(4):
                plane(a, d, 3 + i, mate_p[i], dev_p).wait_recv()

    def exchange(a, own, send, recv, scale):
        for d in range(1, nz):
            zd = (z + d) % nz
            send[zd] = (own[pl.ds(pl.multiple_of(zd * sub, sub), sub), :] * scale).astype(PART)
            go(remote(send.at[zd], recv.at[z], ls_sem.at[a, d - 1], lr_sem.at[a, d - 1], (g, zd, r)))

    def collect(a, own, recv, scale):
        total = own[pl.ds(pl.multiple_of(z * sub, sub), sub), :]
        for d in range(1, nz):
            zd = (z - d) % nz
            dst = recv.at[zd]
            remote(dst, dst, ls_sem.at[a, d - 1], lr_sem.at[a, d - 1], (g, zd, r)).wait_recv()
            total = total + recv[zd].astype(jnp.float32) * (1.0 / scale)
        return total

    stage1(0)
    stage1(1)
    stage2(0)
    stage3(0)
    stage2(1)
    stage4(0)
    loc_s.wait()
    own_s[...] = jnp.dot(sht[...], ws[...], preferred_element_type=jnp.float32)
    scale_s = part_scale(fs)
    exchange(0, own_s, send_s, recv_s, scale_s)
    stage3(1)

    for i, q in enumerate(row_peers):
        dst = pick_all.at[q]
        remote(dst, dst, ks_sem.at[i], kr_sem.at[i], (g, z, q)).wait_recv()
    picks = jnp.zeros_like(pick_ref)
    for b in range(4):
        picks = jnp.where(bmask_ref[b] > 0.5, pick_all[b], picks)
    pick_t = jnp.broadcast_to(picks[0:1], (128, picks.shape[1])).T[:, 0:1]

    stage4(1)
    loc_t.wait()
    logits = jnp.zeros(own_t.shape, jnp.float32)
    for t in range(wt.shape[0]):
        one = jnp.dot(tht[...], wt[t], preferred_element_type=jnp.float32)
        logits = jnp.where(jnp.abs(pick_t - t) < 0.5, one, logits)
    own_t[...] = logits
    scale_t = part_scale(ft)
    exchange(1, own_t, send_t, recv_t, scale_t)

    student = collect(0, own_s, recv_s, scale_s)
    s_shift = student - jnp.max(student, axis=1, keepdims=True)
    log_s = s_shift - jnp.log(jnp.sum(jnp.exp(s_shift), axis=1, keepdims=True))
    p_s = jnp.exp(log_s)

    tl_all[r] = collect(1, own_t, recv_t, scale_t)
    for i, q in enumerate(row_peers):
        go(remote(tl_all.at[r], tl_all.at[r], rs_sem.at[i], rr_sem.at[i], (g, z, q)))
    for i, q in enumerate(row_peers):
        dst = tl_all.at[q]
        remote(dst, dst, rs_sem.at[i], rr_sem.at[i], (g, z, q)).wait_recv()
    teacher = tl_all[0]
    for j in range(1, 4):
        teacher = jnp.where(smask_ref[j, 0:1, :] > 0.5, tl_all[j], teacher)

    t_shift = teacher - jnp.max(teacher, axis=1, keepdims=True)
    log_t = t_shift - jnp.log(jnp.sum(jnp.exp(t_shift), axis=1, keepdims=True))
    p_t = jnp.exp(log_t)
    diff = log_s - log_t
    fkl = -jnp.sum(p_t * diff, axis=1, keepdims=True)
    rkl = jnp.sum(p_s * diff, axis=1, keepdims=True)
    dz_all[z] = ((p_s - p_t) + p_s * (diff - rkl)).astype(jnp.bfloat16)
    lane = lax.broadcasted_iota(jnp.int32, (sub, 128), 1)
    both = jnp.where(lane == 0, fkl, rkl)
    kl_all[z] = both.T[0:8, :]

    for d in range(1, nz):
        zd = (z + d) % nz
        go(remote(dz_all.at[z], dz_all.at[z], ds_sem.at[0, d - 1], dr_sem.at[0, d - 1], (g, zd, r)))
        go(remote(kl_all.at[z], kl_all.at[z], ds_sem.at[1, d - 1], dr_sem.at[1, d - 1], (g, zd, r)))
    for d in range(1, nz):
        zd = (z - d) % nz
        for a, ref in ((0, dz_all), (1, kl_all)):
            dst = ref.at[zd]
            remote(dst, dst, ds_sem.at[a, d - 1], dr_sem.at[a, d - 1], (g, zd, r)).wait_recv()
    for q in range(nz):
        kl_ref[q] = kl_all[q]
    dz = dz_all[...].reshape(nz * sub, dz_all.shape[2])
    grad_ref[...] = lax.dot_general(
        ws[...], dz, (((1,), (1,)), ((), ())), preferred_element_type=jnp.float32
    ).astype(jnp.bfloat16)
    for copy in sends:
        copy.wait_send()


def local_fast(student_hidden, teacher_hidden, teacher_head, student_head, teacher_pick, owner):
    nz = lax.axis_size("vocab")
    n_rows = lax.axis_size("rows")
    fs, rows = student_hidden.shape
    ft = teacher_hidden.shape[0]
    teachers, _, vl = teacher_head.shape
    sub = rows // owner.shape[0]
    vocab = vl * nz
    r = lax.axis_index("rows")
    z = lax.axis_index("vocab")
    ranks = jnp.arange(n_rows, dtype=jnp.int32)
    pick = jnp.broadcast_to(teacher_pick.astype(jnp.float32)[None, :], (8, rows))
    goes_to = jnp.repeat(lax.dynamic_index_in_dim(owner, r, 1, keepdims=False), sub)
    bmask = jnp.broadcast_to(
        (goes_to[None, None, :] == ranks[:, None, None]).astype(jnp.float32), (n_rows, 8, rows)
    )
    comes = (lax.dynamic_index_in_dim(owner, z, 0, keepdims=False) == r).astype(jnp.float32)
    smask = jnp.broadcast_to(comes[:, None, None], (n_rows, 8, vocab))
    vmem = pl.BlockSpec(memory_space=pltpu.VMEM)
    hbm = pl.BlockSpec(memory_space=pl.ANY)
    dma = pltpu.SemaphoreType.DMA
    kl, grad = pl.pallas_call(
        functools.partial(window_kernel, nz, sub),
        out_shape=(
            jax.ShapeDtypeStruct((nz, 8, sub), jnp.float32),
            jax.ShapeDtypeStruct((fs, rows), jnp.bfloat16),
        ),
        in_specs=[vmem, vmem, hbm, hbm, vmem, vmem, vmem],
        out_specs=(vmem, vmem),
        scratch_shapes=[
            pltpu.VMEM((teachers, ft, vocab), jnp.bfloat16),
            pltpu.VMEM((fs, vocab), jnp.bfloat16),
            pltpu.VMEM((rows, fs), jnp.bfloat16),
            pltpu.VMEM((rows, ft), jnp.bfloat16),
            pltpu.VMEM((rows, vocab), jnp.float32),
            pltpu.VMEM((rows, vocab), jnp.float32),
            pltpu.VMEM((nz, sub, vocab), PART),
            pltpu.VMEM((nz, sub, vocab), PART),
            pltpu.VMEM((nz, sub, vocab), PART),
            pltpu.VMEM((nz, sub, vocab), PART),
            pltpu.VMEM((n_rows, sub, vocab), jnp.float32),
            pltpu.VMEM((nz, sub, vocab), jnp.bfloat16),
            pltpu.VMEM((nz, 8, sub), jnp.float32),
            pltpu.VMEM((n_rows, 8, rows), jnp.float32),
            dma((2,)),
            dma((2, nz - 1)),
            dma((2, nz - 1)),
            dma((2, nz - 1, 7)),
            dma((2, nz - 1, 7)),
            dma((3,)),
            dma((3,)),
            dma((2, nz - 1)),
            dma((2, nz - 1)),
            dma((3,)),
            dma((3,)),
            dma((2, nz - 1)),
            dma((2, nz - 1)),
        ],
        compiler_params=pltpu.CompilerParams(
            collective_id=0, has_side_effects=True, vmem_limit_bytes=40 * 1024 * 1024
        ),
    )(student_hidden, teacher_hidden, teacher_head, student_head, pick, bmask, smask)
    return kl[:, 0, :].reshape(rows), kl[:, 1, :].reshape(rows), grad


def local_any(student_hidden, teacher_hidden, teacher_head, student_head, teacher_pick, owner):
    rows_local = student_hidden.shape[1]
    round_count = owner.shape[0]
    sub_rows = rows_local // round_count
    row_devices = lax.axis_size("rows")
    own_rank = lax.axis_index("rows")
    all_ranks = jnp.arange(row_devices, dtype=jnp.int32)
    routed_parts = []
    for round_id in range(round_count):
        row_block = teacher_hidden[:, round_id * sub_rows : (round_id + 1) * sub_rows]
        gathered = lax.all_gather(row_block, "rows", axis=1, tiled=True)
        source = jnp.sum(jnp.where(owner[round_id] == own_rank, all_ranks, 0))
        routed_parts.append(lax.dynamic_slice_in_dim(gathered, source * sub_rows, sub_rows, 1))
    routed = jnp.concatenate(routed_parts, axis=1)
    teacher_count = teacher_head.shape[0]
    row_order = jnp.argsort(teacher_pick, stable=True)
    back_order = jnp.argsort(row_order, stable=True)
    group_sizes = jnp.sum(
        (teacher_pick[None, :] == jnp.arange(teacher_count, dtype=jnp.int32)[:, None]).astype(
            jnp.int32
        ),
        axis=1,
    )
    routed_sorted = routed[:, row_order]
    voc_local = student_head.shape[1]
    empty_logits = jnp.zeros((rows_local, voc_local), jnp.float32)
    head_rows = teacher_head
    sorted_logits = empty_logits + lax.ragged_dot(
        lax.all_gather(routed_sorted, "vocab", axis=0, tiled=True).T,
        head_rows,
        group_sizes,
        preferred_element_type=jnp.float32,
    )
    teacher_logits = sorted_logits[back_order]
    head_rows = student_head
    student_logits = lax.dot_general(
        lax.all_gather(student_hidden, "vocab", axis=0, tiled=True),
        head_rows,
        (((0,), (0,)), ((), ())),
        preferred_element_type=jnp.float32,
    )
    t_peak, s_peak = lax.pmax(
        (jnp.max(teacher_logits, axis=1), jnp.max(student_logits, axis=1)), "vocab"
    )
    t_total, s_total = lax.psum(
        (
            jnp.sum(jnp.exp(teacher_logits - t_peak[:, None]), axis=1),
            jnp.sum(jnp.exp(student_logits - s_peak[:, None]), axis=1),
        ),
        "vocab",
    )
    log_teacher = teacher_logits - (t_peak + jnp.log(t_total))[:, None]
    log_student = student_logits - (s_peak + jnp.log(s_total))[:, None]
    p_teacher = jnp.exp(log_teacher)
    p_student = jnp.exp(log_student)
    forward_kl, reverse_kl = lax.psum(
        (
            jnp.sum(p_teacher * (log_teacher - log_student), axis=1),
            jnp.sum(p_student * (log_student - log_teacher), axis=1),
        ),
        "vocab",
    )
    logit_grad = (
        p_student - p_teacher + p_student * (log_student - log_teacher - reverse_kl[:, None])
    ).astype(jnp.bfloat16)
    out_rows = student_head.shape[0] // lax.axis_size("vocab")
    head_rows = student_head
    grad_all = lax.psum(
        lax.dot_general(
            head_rows, logit_grad, (((1,), (1,)), ((), ())), preferred_element_type=jnp.float32
        ),
        "vocab",
    )
    grad_hidden = lax.dynamic_slice_in_dim(
        grad_all, lax.axis_index("vocab") * out_rows, out_rows, 0
    )
    return (forward_kl, reverse_kl, grad_hidden.astype(jnp.bfloat16))


def solution(mesh):
    placed = (
        P("vocab", ("groups", "rows")),
        P("vocab", ("groups", "rows")),
        P(None, None, "vocab"),
        P(None, "vocab"),
        P(("groups", "rows")),
        P("groups", None),
    )

    def local(student_hidden, teacher_hidden, teacher_head, student_head, teacher_pick, owner):
        args = (student_hidden, teacher_hidden, teacher_head, student_head, teacher_pick, owner)
        sizes = (mesh.shape["groups"], mesh.shape["rows"], mesh.shape["vocab"])
        fits = sizes == (2, 4, owner.shape[0]) and student_hidden.shape[0] % 128 == 0
        return (local_fast if fits else local_any)(*args)

    return jax.shard_map(
        local,
        mesh=mesh,
        in_specs=placed,
        out_specs=(P(("groups", "rows")), P(("groups", "rows")), P("vocab", ("groups", "rows"))),
        check_vma=False,
    )
```

```python
import functools
import math

import jax
import jax.numpy as jnp
from jax import lax
from jax.experimental import pallas as pl
from jax.experimental.pallas import tpu as pltpu
from jax.sharding import PartitionSpec as P

MESH = pl.DeviceIdType.MESH
CODE_TOP = 32760.0
CODE_UNIT = 4.0


def code_range(x):
    top = jnp.maximum(jnp.max(jnp.max(jnp.abs(x), axis=1, keepdims=True), axis=0, keepdims=True), 0.01)
    top = top * (1.0 / CODE_UNIT)
    return jnp.log(top + jnp.sqrt(top * top + 1.0))


def encode(x, span):
    y = jnp.abs(x) * (1.0 / CODE_UNIT)
    y = jnp.log(y + jnp.sqrt(y * y + 1.0)) * (CODE_TOP / span) + 0.5
    return jnp.where(x < 0, -y, y).astype(jnp.int32).astype(jnp.int16)


def decode(code, span):
    e = jnp.exp(code.astype(jnp.float32) * (span * (1.0 / CODE_TOP)))
    return (e - 1.0 / e) * (0.5 * CODE_UNIT)


def window_kernel(
    nz,
    sub,
    sh_hbm,
    th_hbm,
    thead_ref,
    shead_ref,
    pick_ref,
    owner_ref,
    kl_ref,
    grad_ref,
    sh_ref,
    th_ref,
    wt,
    ws,
    sht,
    tht,
    own_t,
    own_s,
    send_t,
    send_s,
    recv_t,
    recv_s,
    meta_send,
    meta_recv,
    tl_all,
    tm_all,
    dz_all,
    kl_all,
    pick_all,
    local_sem,
    zs_sem,
    zr_sem,
    ps_sem,
    pr_sem,
    ks_sem,
    kr_sem,
    ls_sem,
    lr_sem,
    rs_sem,
    rr_sem,
    ds_sem,
    dr_sem,
):
    g = lax.axis_index("groups")
    z = lax.axis_index("vocab")
    r = lax.axis_index("rows")
    x, c = r // 2, r % 2
    rx = (1 - x) * 2 + c
    rp = x * 2 + (1 - c)
    ro = (1 - x) * 2 + (1 - c)
    gy = 1 - g
    dev_x, dev_y, dev_p = (g, z, rx), (gy, z, r), (g, z, rp)
    row_peers = (rp, rx, ro)
    own_p = (g * 4 + r, g * 4 + rx, gy * 4 + r, gy * 4 + rx)
    mate_p = (g * 4 + rp, g * 4 + ro, gy * 4 + rp, gy * 4 + ro)
    fwd_p = jnp.where(c == 0, own_p[1], own_p[2])
    fwd_dev = (jnp.where(c == 0, gy, g), z, jnp.where(c == 0, r, rx))

    ft, fs = th_ref.shape[0], sh_ref.shape[0]
    bt, bs = ft // 8, fs // 8
    vl = thead_ref.shape[2]

    def at(a, piece, zz):
        cols = pl.ds(pl.multiple_of(zz * vl, vl), vl)
        if a == 0:
            return ws.at[pl.ds(pl.multiple_of(piece * bs, bs), bs), cols]
        return wt.at[a - 1, pl.ds(pl.multiple_of(piece * bt, bt), bt), cols]

    def head_at(a, zz):
        if a == 0:
            return shead_ref.at[pl.ds(pl.multiple_of(zz * fs + own_p[0] * bs, bs), bs), :]
        return thead_ref.at[a - 1, pl.ds(pl.multiple_of(zz * ft + own_p[0] * bt, bt), bt), :]

    def remote(src, dst, ssem, rsem, dev):
        return pltpu.make_async_remote_copy(
            src_ref=src, dst_ref=dst, send_sem=ssem, recv_sem=rsem, device_id=dev, device_id_type=MESH
        )

    loc_t = pltpu.make_async_copy(
        thead_ref.at[:, pl.ds(pl.multiple_of(z * ft, ft), ft), :],
        wt.at[:, :, pl.ds(pl.multiple_of(z * vl, vl), vl)],
        local_sem.at[0],
    )
    loc_s = pltpu.make_async_copy(
        shead_ref.at[pl.ds(pl.multiple_of(z * fs, fs), fs), :],
        ws.at[:, pl.ds(pl.multiple_of(z * vl, vl), vl)],
        local_sem.at[1],
    )
    loc_sh = pltpu.make_async_copy(sh_hbm, sh_ref, local_sem.at[2])
    loc_th = pltpu.make_async_copy(th_hbm, th_ref, local_sem.at[3])

    barrier = pltpu.get_barrier_semaphore()
    peers = [(g, (z + d) % nz, r) for d in range(1, nz)]
    peers += [(g, z, q) for q in row_peers] + [dev_y]
    for dev in peers:
        pl.semaphore_signal(barrier, inc=1, device_id=dev, device_id_type=MESH)
    pl.semaphore_wait(barrier, len(peers))

    sends = []

    def go(copy):
        copy.start()
        sends.append(copy)

    def stage0(a):
        for d in range(1, nz):
            zd = (z + d) % nz
            go(
                remote(
                    head_at(a, zd),
                    at(a, own_p[0], z),
                    zs_sem.at[a, d - 1],
                    zr_sem.at[a, d - 1],
                    (g, zd, r),
                )
            )

    stage0(0)
    stage0(1)
    stage0(2)
    loc_sh.start()
    loc_th.start()
    loc_s.start()
    loc_t.start()
    pick_all[r] = jnp.broadcast_to(pick_ref[...], pick_all.shape[1:])
    for i, q in enumerate(row_peers):
        go(remote(pick_all.at[r], pick_all.at[r], ks_sem.at[i], kr_sem.at[i], (g, z, q)))

    loc_sh.wait()
    sht[...] = sh_ref[...].T
    loc_th.wait()
    tht[...] = th_ref[...].T

    def plane(a, d, kind, piece, dev):
        ref = at(a, piece, (z - d) % nz)
        return remote(ref, ref, ps_sem.at[a, d - 1, kind], pr_sem.at[a, d - 1, kind], dev)

    def stage1(a):
        for d in range(1, nz):
            zd = (z - d) % nz
            dst = at(a, own_p[0], zd)
            remote(dst, dst, zs_sem.at[a, d - 1], zr_sem.at[a, d - 1], (g, zd, r)).wait_recv()
            go(plane(a, d, 0, own_p[0], dev_x))
            go(plane(a, d, 1, own_p[0], dev_y))
            go(plane(a, d, 3, own_p[0], dev_p))

    def stage2(a):
        for d in range(1, nz):
            plane(a, d, 0, own_p[1], dev_x).wait_recv()
            plane(a, d, 1, own_p[2], dev_y).wait_recv()
            go(plane(a, d, 2, fwd_p, fwd_dev))
            go(plane(a, d, 4, own_p[1], dev_p))
            go(plane(a, d, 5, own_p[2], dev_p))

    def stage3(a):
        for d in range(1, nz):
            plane(a, d, 2, own_p[3], dev_x).wait_recv()
            go(plane(a, d, 6, own_p[3], dev_p))

    def stage4(a):
        for d in range(1, nz):
            for i in range(4):
                plane(a, d, 3 + i, mate_p[i], dev_p).wait_recv()

    def exchange(a, own, send, recv):
        for d in range(1, nz):
            zd = (z + d) % nz
            part = own[pl.ds(pl.multiple_of(zd * sub, sub), sub), :]
            span = code_range(part)
            send[zd] = encode(part, span)
            meta_send[a, zd] = jnp.broadcast_to(span, meta_send.shape[2:])
            dev = (g, zd, r)
            go(remote(send.at[zd], recv.at[z], ls_sem.at[a, d - 1], lr_sem.at[a, d - 1], dev))
            go(
                remote(
                    meta_send.at[a, zd],
                    meta_recv.at[a, z],
                    ls_sem.at[2 + a, d - 1],
                    lr_sem.at[2 + a, d - 1],
                    dev,
                )
            )

    def collect(a, own, recv):
        total = own[pl.ds(pl.multiple_of(z * sub, sub), sub), :]
        for d in range(1, nz):
            zd = (z - d) % nz
            dst, meta = recv.at[zd], meta_recv.at[a, zd]
            dev = (g, zd, r)
            remote(dst, dst, ls_sem.at[a, d - 1], lr_sem.at[a, d - 1], dev).wait_recv()
            remote(meta, meta, ls_sem.at[2 + a, d - 1], lr_sem.at[2 + a, d - 1], dev).wait_recv()
            total = total + decode(recv[zd], meta_recv[a, zd][0:1, 0:1])
        return total

    stage1(0)
    stage1(1)
    stage0(3)
    stage2(0)
    stage2(1)
    stage3(0)
    stage1(2)
    stage3(1)
    stage2(2)
    stage4(0)
    loc_s.wait()
    own_s[...] = jnp.dot(sht[...], ws[...], preferred_element_type=jnp.float32)
    stage1(3)
    stage3(2)
    stage2(3)
    exchange(0, own_s, send_s, recv_s)

    for i, q in enumerate(row_peers):
        dst = pick_all.at[q]
        remote(dst, dst, ks_sem.at[i], kr_sem.at[i], (g, z, q)).wait_recv()
    lanes = lax.broadcasted_iota(jnp.int32, pick_all.shape[1:], 1)
    goes_to = jnp.zeros_like(lanes)
    for k in range(nz):
        goes_to = jnp.where(lanes >= k * sub, owner_ref[k, r], goes_to)
    picks = jnp.zeros_like(lanes)
    for b in range(4):
        picks = jnp.where(goes_to == b, pick_all[b], picks)
    picks = picks.astype(jnp.float32)
    pick_t = jnp.broadcast_to(picks[0:1], (128, picks.shape[1])).T[:, 0:1]

    loc_t.wait()
    for t in range(wt.shape[0]):
        if t == wt.shape[0] - 1:
            stage3(t + 1)
        stage4(t + 1)
        one = jnp.dot(tht[...], wt[t], preferred_element_type=jnp.float32)
        own_t[...] = one if t == 0 else jnp.where(jnp.abs(pick_t - t) < 0.5, one, own_t[...])
    exchange(1, own_t, send_t, recv_t)

    student = collect(0, own_s, recv_s)
    s_shift = student - jnp.max(student, axis=1, keepdims=True)
    log_s = s_shift - jnp.log(jnp.sum(jnp.exp(s_shift), axis=1, keepdims=True))
    p_s = jnp.exp(log_s)

    reduced = collect(1, own_t, recv_t)
    span = code_range(reduced)
    tl_all[r] = encode(reduced, span)
    tm_all[r] = jnp.broadcast_to(span, tm_all.shape[1:])
    for i, q in enumerate(row_peers):
        for a, ref in ((0, tl_all), (1, tm_all)):
            go(remote(ref.at[r], ref.at[r], rs_sem.at[a, i], rr_sem.at[a, i], (g, z, q)))
    for i, q in enumerate(row_peers):
        for a, ref in ((0, tl_all), (1, tm_all)):
            dst = ref.at[q]
            remote(dst, dst, rs_sem.at[a, i], rr_sem.at[a, i], (g, z, q)).wait_recv()
    wanted, span = tl_all[0].astype(jnp.int32), tm_all[0][0:1, 0:1]
    for j in range(1, 4):
        comes = owner_ref[z, j]
        wanted = jnp.where(jnp.zeros_like(wanted) + comes == r, tl_all[j].astype(jnp.int32), wanted)
        span = jnp.where(jnp.zeros((1, 1), jnp.int32) + comes == r, tm_all[j][0:1, 0:1], span)
    teacher = decode(wanted, span)

    t_shift = teacher - jnp.max(teacher, axis=1, keepdims=True)
    log_t = t_shift - jnp.log(jnp.sum(jnp.exp(t_shift), axis=1, keepdims=True))
    p_t = jnp.exp(log_t)
    diff = log_s - log_t
    fkl = -jnp.sum(p_t * diff, axis=1, keepdims=True)
    rkl = jnp.sum(p_s * diff, axis=1, keepdims=True)
    dz_all[z] = ((p_s - p_t) + p_s * (diff - rkl)).astype(jnp.bfloat16)
    lane = lax.broadcasted_iota(jnp.int32, (sub, 128), 1)
    both = jnp.where(lane == 0, fkl, rkl)
    kl_all[z] = both.T[0:8, :]

    for d in range(1, nz):
        zd = (z + d) % nz
        go(remote(dz_all.at[z], dz_all.at[z], ds_sem.at[0, d - 1], dr_sem.at[0, d - 1], (g, zd, r)))
        go(remote(kl_all.at[z], kl_all.at[z], ds_sem.at[1, d - 1], dr_sem.at[1, d - 1], (g, zd, r)))
    for d in range(1, nz):
        zd = (z - d) % nz
        for a, ref in ((0, dz_all), (1, kl_all)):
            dst = ref.at[zd]
            remote(dst, dst, ds_sem.at[a, d - 1], dr_sem.at[a, d - 1], (g, zd, r)).wait_recv()
    for q in range(nz):
        kl_ref[q] = kl_all[q]
    dz = dz_all[...].reshape(nz * sub, dz_all.shape[2])
    grad_ref[...] = lax.dot_general(
        ws[...], dz, (((1,), (1,)), ((), ())), preferred_element_type=jnp.float32
    ).astype(jnp.bfloat16)
    for copy in sends:
        copy.wait_send()


def local_fast(student_hidden, teacher_hidden, teacher_head, student_head, teacher_pick, owner):
    nz = lax.axis_size("vocab")
    n_rows = lax.axis_size("rows")
    fs, rows = student_hidden.shape
    ft = teacher_hidden.shape[0]
    teachers, _, vl = teacher_head.shape
    sub = rows // owner.shape[0]
    vocab = vl * nz
    vmem = pl.BlockSpec(memory_space=pltpu.VMEM)
    hbm = pl.BlockSpec(memory_space=pl.ANY)
    dma = pltpu.SemaphoreType.DMA
    kl, grad = pl.pallas_call(
        functools.partial(window_kernel, nz, sub),
        out_shape=(
            jax.ShapeDtypeStruct((nz, 8, sub), jnp.float32),
            jax.ShapeDtypeStruct((fs, rows), jnp.bfloat16),
        ),
        in_specs=[hbm, hbm, hbm, hbm, vmem, pl.BlockSpec(memory_space=pltpu.SMEM)],
        out_specs=(vmem, vmem),
        scratch_shapes=[
            pltpu.VMEM((fs, rows), jnp.bfloat16),
            pltpu.VMEM((ft, rows), jnp.bfloat16),
            pltpu.VMEM((teachers, ft, vocab), jnp.bfloat16),
            pltpu.VMEM((fs, vocab), jnp.bfloat16),
            pltpu.VMEM((rows, fs), jnp.bfloat16),
            pltpu.VMEM((rows, ft), jnp.bfloat16),
            pltpu.VMEM((rows, vocab), jnp.float32),
            pltpu.VMEM((rows, vocab), jnp.float32),
            pltpu.VMEM((nz, sub, vocab), jnp.int16),
            pltpu.VMEM((nz, sub, vocab), jnp.int16),
            pltpu.VMEM((nz, sub, vocab), jnp.int16),
            pltpu.VMEM((nz, sub, vocab), jnp.int16),
            pltpu.VMEM((2, nz, 8, 128), jnp.float32),
            pltpu.VMEM((2, nz, 8, 128), jnp.float32),
            pltpu.VMEM((n_rows, sub, vocab), jnp.int16),
            pltpu.VMEM((n_rows, 8, 128), jnp.float32),
            pltpu.VMEM((nz, sub, vocab), jnp.bfloat16),
            pltpu.VMEM((nz, 8, sub), jnp.float32),
            pltpu.VMEM((n_rows, 8, rows), jnp.int32),
            dma((4,)),
            dma((1 + teachers, nz - 1)),
            dma((1 + teachers, nz - 1)),
            dma((1 + teachers, nz - 1, 7)),
            dma((1 + teachers, nz - 1, 7)),
            dma((3,)),
            dma((3,)),
            dma((4, nz - 1)),
            dma((4, nz - 1)),
            dma((2, 3)),
            dma((2, 3)),
            dma((2, nz - 1)),
            dma((2, nz - 1)),
        ],
        compiler_params=pltpu.CompilerParams(
            collective_id=0, has_side_effects=True, vmem_limit_bytes=58 * 1024 * 1024
        ),
    )(student_hidden, teacher_hidden, teacher_head, student_head, teacher_pick[None, :], owner)
    return kl[:, 0, :].reshape(rows), kl[:, 1, :].reshape(rows), grad


def local_any(student_hidden, teacher_hidden, teacher_head, student_head, teacher_pick, owner):
    rows_local = student_hidden.shape[1]
    round_count = owner.shape[0]
    sub_rows = rows_local // round_count
    row_devices = lax.axis_size("rows")
    own_rank = lax.axis_index("rows")
    all_ranks = jnp.arange(row_devices, dtype=jnp.int32)
    routed_parts = []
    for round_id in range(round_count):
        row_block = teacher_hidden[:, round_id * sub_rows : (round_id + 1) * sub_rows]
        gathered = lax.all_gather(row_block, "rows", axis=1, tiled=True)
        source = jnp.sum(jnp.where(owner[round_id] == own_rank, all_ranks, 0))
        routed_parts.append(lax.dynamic_slice_in_dim(gathered, source * sub_rows, sub_rows, 1))
    routed = jnp.concatenate(routed_parts, axis=1)
    teacher_count = teacher_head.shape[0]
    row_order = jnp.argsort(teacher_pick, stable=True)
    back_order = jnp.argsort(row_order, stable=True)
    group_sizes = jnp.sum(
        (teacher_pick[None, :] == jnp.arange(teacher_count, dtype=jnp.int32)[:, None]).astype(
            jnp.int32
        ),
        axis=1,
    )
    routed_sorted = routed[:, row_order]
    voc_local = student_head.shape[1]
    empty_logits = jnp.zeros((rows_local, voc_local), jnp.float32)
    head_rows = teacher_head
    sorted_logits = empty_logits + lax.ragged_dot(
        lax.all_gather(routed_sorted, "vocab", axis=0, tiled=True).T,
        head_rows,
        group_sizes,
        preferred_element_type=jnp.float32,
    )
    teacher_logits = sorted_logits[back_order]
    head_rows = student_head
    student_logits = lax.dot_general(
        lax.all_gather(student_hidden, "vocab", axis=0, tiled=True),
        head_rows,
        (((0,), (0,)), ((), ())),
        preferred_element_type=jnp.float32,
    )
    t_peak, s_peak = lax.pmax(
        (jnp.max(teacher_logits, axis=1), jnp.max(student_logits, axis=1)), "vocab"
    )
    t_total, s_total = lax.psum(
        (
            jnp.sum(jnp.exp(teacher_logits - t_peak[:, None]), axis=1),
            jnp.sum(jnp.exp(student_logits - s_peak[:, None]), axis=1),
        ),
        "vocab",
    )
    log_teacher = teacher_logits - (t_peak + jnp.log(t_total))[:, None]
    log_student = student_logits - (s_peak + jnp.log(s_total))[:, None]
    p_teacher = jnp.exp(log_teacher)
    p_student = jnp.exp(log_student)
    forward_kl, reverse_kl = lax.psum(
        (
            jnp.sum(p_teacher * (log_teacher - log_student), axis=1),
            jnp.sum(p_student * (log_student - log_teacher), axis=1),
        ),
        "vocab",
    )
    logit_grad = (
        p_student - p_teacher + p_student * (log_student - log_teacher - reverse_kl[:, None])
    ).astype(jnp.bfloat16)
    out_rows = student_head.shape[0] // lax.axis_size("vocab")
    head_rows = student_head
    grad_all = lax.psum(
        lax.dot_general(
            head_rows, logit_grad, (((1,), (1,)), ((), ())), preferred_element_type=jnp.float32
        ),
        "vocab",
    )
    grad_hidden = lax.dynamic_slice_in_dim(
        grad_all, lax.axis_index("vocab") * out_rows, out_rows, 0
    )
    return (forward_kl, reverse_kl, grad_hidden.astype(jnp.bfloat16))


def solution(mesh):
    placed = (
        P("vocab", ("groups", "rows")),
        P("vocab", ("groups", "rows")),
        P(None, None, "vocab"),
        P(None, "vocab"),
        P(("groups", "rows")),
        P("groups", None),
    )

    def local(student_hidden, teacher_hidden, teacher_head, student_head, teacher_pick, owner):
        args = (student_hidden, teacher_hidden, teacher_head, student_head, teacher_pick, owner)
        sizes = (mesh.shape["groups"], mesh.shape["rows"], mesh.shape["vocab"])
        fits = sizes == (2, 4, owner.shape[0]) and teacher_head.shape[0] == 3
        return (local_fast if fits else local_any)(*args)

    return jax.shard_map(
        local,
        mesh=mesh,
        in_specs=placed,
        out_specs=(P(("groups", "rows")), P(("groups", "rows")), P("vocab", ("groups", "rows"))),
        check_vma=False,
    )
```
